512 devices in a mesh: tm: 64 (over y, z_hi, x, core), head: 8 (over z_lo).
Axes of the slice: x: 4, y: 4, z: 16 (z_hi: 2, z_lo: 8; z = z_hi * 8 + z_lo), core: 2. Of those that a mesh axis runs over, the one named last changes fastest.
Arguments:
- queries: bfloat16 [64, 392, 1024], P('tm', None, 'head'), may hold values from -6 to 6
- key_tokens: bfloat16 [64, 392, 1024], P('tm', None, 'head'), may hold values from -6 to 6
- value_tokens: bfloat16 [64, 392, 1024], P('tm', None, 'head'), may hold values from -6 to 6
- out_weight: bfloat16 [1024, 1024], P('head'), may hold values from -0.1875 to 0.1875
- out_grad: bfloat16 [64, 392, 1024], P('tm'), may hold values from -6 to 6
- clip_starts: int32 [64], P('tm'), may hold values from 0 to 1, as said below
Outputs:
- projected: bfloat16 [64, 392, 1024], P('tm', 'head')
- grad_queries: bfloat16 [64, 392, 1024], P('tm', None, 'head')
- grad_keys: bfloat16 [64, 392, 1024], P('tm', None, 'head')
- grad_values: bfloat16 [64, 392, 1024], P('tm', None, 'head')
The draws below stay inside these ranges and needn't reach their ends.
Inputs may be any that keep to these rules, and one draw needn't show every extreme that they name: `clip_starts`: the last 8 clips never begin a new video.
All inputs are finite; a program needn't handle non-finite values.
Results may differ from the reference program's by a relative error of at most 0.0087.
Values may be sent and summed in bfloat16 or wider, within the bound.
No kernel may reach another device: no remote copies, remote signals or barrier semaphores. Data moves between devices by JAX's collectives and lax.ppermute only.
A program may use at most 64 MiB of HBM per device.

```python
import jax
import jax.numpy as jnp
from jax import lax

HEADS = 16
HEAD_DIM = 64
WIDTH = 1024
TOK = 392
POOL = 4
MEM = 8
CLIPS = 64


def base_field(key, seed_tag):
    return jax.random.truncated_normal(jax.random.fold_in(key, seed_tag), -6.0, 6.0, (CLIPS, TOK, WIDTH), jnp.float32)


def draw_queries(key, part):
    field = base_field(key, 1)
    return field.astype(jnp.bfloat16)


def draw_key_tokens(key, part):
    field = base_field(key, 2)
    return field.astype(jnp.bfloat16)


def draw_clip_starts(key, part):
    dice = jax.random.randint(jax.random.fold_in(key, 21), (CLIPS,), 0, 4)
    forced = jax.random.randint(jax.random.fold_in(key, 22), (), 0, CLIPS - MEM)
    positions = jnp.arange(CLIPS)
    starts = jnp.where((dice == 0) | (positions == forced), 1, 0).astype(jnp.int32)
    late = positions >= CLIPS - MEM
    return jnp.where(late, 0, starts).astype(jnp.int32)


def levels(own_key, shape, pieces, least, high):
    loudness = 1.0
    for dim, parts in pieces:
        steps = jax.random.uniform(jax.random.fold_in(jax.random.fold_in(own_key, 6), dim), (parts,), jnp.float32, least / len(pieces), high / len(pieces))
        loudness = loudness * jnp.repeat(jnp.exp(steps), shape[dim] // parts).reshape((-1,) + (1,) * (len(shape) - 1 - dim))
    return loudness


def noise(key, shape, deviation, reach, pieces=(), held_as=jnp.bfloat16):
    loudness = levels(key, shape, pieces, -0.22, 0.18) if pieces else 1.0
    result = jax.random.normal(key, shape, jnp.float32) * deviation * loudness
    return jnp.minimum(jnp.maximum(result, -reach), reach).astype(held_as)


def setup_inputs(seed: int = 0) -> dict:
    key_list = jax.random.split(jax.random.key(seed), 7)
    return {
        "queries": draw_queries(jax.random.fold_in(key_list[6], 71), 0),
        "key_tokens": draw_key_tokens(jax.random.fold_in(key_list[6], 71), 0),
        "value_tokens": noise(key_list[2], (CLIPS, TOK, WIDTH), 1.0, 6.0, ((0, 64), (2, 8))),
        "out_weight": noise(key_list[3], (WIDTH, WIDTH), WIDTH ** -0.5, 0.1875, ((0, 8),)),
        "out_grad": noise(key_list[4], (CLIPS, TOK, WIDTH), 1.0, 6.0, ((0, 64),)),
        "clip_starts": draw_clip_starts(jax.random.fold_in(key_list[6], 71), 0),
    }


def delayed(series, places):
    return jnp.concatenate([jnp.zeros((places,), series.dtype), series[:series.shape[0] - places]])


def clip_terms(query_clip, key_ext, value_ext, column_mask, grad_clip):
    scale = HEAD_DIM ** -0.5
    query_heads = query_clip.astype(jnp.float32).reshape(TOK, HEADS, HEAD_DIM)
    key_heads = key_ext.astype(jnp.float32).reshape(-1, HEADS, HEAD_DIM)
    value_heads = value_ext.astype(jnp.float32).reshape(-1, HEADS, HEAD_DIM)
    grad_heads = grad_clip.astype(jnp.float32).reshape(TOK, HEADS, HEAD_DIM)
    scores = jnp.einsum('qhd,khd->hqk', query_heads, key_heads) * scale
    scores = jnp.where(column_mask[None, None, :] > 0, scores, -1e30)
    peak = jnp.max(scores, axis=-1, keepdims=True)
    expo = jnp.exp(scores - peak)
    probs = expo / jnp.sum(expo, axis=-1, keepdims=True)
    weights = lax.optimization_barrier(probs.astype(jnp.bfloat16)).astype(jnp.float32)
    attended = jnp.einsum('hqk,khd->qhd', weights, value_heads).reshape(TOK, WIDTH).astype(jnp.bfloat16)
    grad_probs = jnp.einsum('qhd,khd->hqk', grad_heads, value_heads)
    delta = jnp.sum(probs * grad_probs, axis=-1, keepdims=True)
    grad_scores = (probs * (grad_probs - delta) * scale).astype(jnp.bfloat16)
    grad_scores = lax.optimization_barrier(grad_scores).astype(jnp.float32)
    grad_query = jnp.einsum('hqk,khd->qhd', grad_scores, key_heads).reshape(TOK, WIDTH).astype(jnp.bfloat16)
    grad_key = jnp.einsum('hqk,qhd->khd', grad_scores, query_heads).reshape(-1, WIDTH)
    grad_value = jnp.einsum('hqk,qhd->khd', weights, grad_heads).reshape(-1, WIDTH)
    return attended, grad_query, grad_key, grad_value


def reference(queries, key_tokens, value_tokens, out_weight, out_grad, clip_starts):
    clips = queries.shape[0]
    pooled_count = TOK // POOL
    pooled_keys = key_tokens.astype(jnp.float32).reshape(clips, pooled_count, POOL, WIDTH).mean(axis=2).astype(jnp.bfloat16)
    pooled_values = value_tokens.astype(jnp.float32).reshape(clips, pooled_count, POOL, WIDTH).mean(axis=2).astype(jnp.bfloat16)
    keep = (1 - clip_starts).astype(jnp.float32)
    present = jnp.ones((clips,), jnp.float32)
    running = keep
    allowed_list = []
    for distance in range(1, MEM + 1):
        allowed_list.append(running * delayed(present, distance))
        running = running * delayed(keep, distance)
    allowed = jnp.stack(allowed_list, axis=1)
    grad_attended = jnp.dot(out_grad.reshape(clips * TOK, WIDTH), out_weight.T, preferred_element_type=jnp.float32)
    grad_attended = grad_attended.astype(jnp.bfloat16).reshape(clips, TOK, WIDTH)
    sources = jnp.maximum(jnp.arange(clips)[:, None] - jnp.arange(1, MEM + 1)[None, :], 0).astype(jnp.int32)

    def per_clip(position):
        memory_keys = pooled_keys[sources[position]].reshape(MEM * pooled_count, WIDTH)
        memory_values = pooled_values[sources[position]].reshape(MEM * pooled_count, WIDTH)
        key_ext = jnp.concatenate([key_tokens[position], memory_keys], axis=0)
        value_ext = jnp.concatenate([value_tokens[position], memory_values], axis=0)
        column_mask = jnp.concatenate([jnp.ones((TOK,), jnp.float32), jnp.repeat(allowed[position], pooled_count)])
        return clip_terms(queries[position], key_ext, value_ext, column_mask, grad_attended[position])

    attended, grad_queries, grad_key_ext, grad_value_ext = lax.map(per_clip, jnp.arange(clips))
    memory_key_grads = grad_key_ext[:, TOK:].reshape(clips, MEM, pooled_count, WIDTH)
    memory_value_grads = grad_value_ext[:, TOK:].reshape(clips, MEM, pooled_count, WIDTH)
    returned_keys = jnp.zeros((clips, pooled_count, WIDTH), jnp.float32)
    returned_values = jnp.zeros((clips, pooled_count, WIDTH), jnp.float32)
    for distance in range(1, MEM + 1):
        padding = jnp.zeros((distance, pooled_count, WIDTH), jnp.float32)
        returned_keys = returned_keys + jnp.concatenate([memory_key_grads[distance:, distance - 1], padding], axis=0)
        returned_values = returned_values + jnp.concatenate([memory_value_grads[distance:, distance - 1], padding], axis=0)
    grad_keys = (grad_key_ext[:, :TOK] + jnp.repeat(returned_keys, POOL, axis=1) / POOL).astype(jnp.bfloat16)
    grad_values = (grad_value_ext[:, :TOK] + jnp.repeat(returned_values, POOL, axis=1) / POOL).astype(jnp.bfloat16)
    projected = jnp.dot(attended.reshape(clips * TOK, WIDTH), out_weight, preferred_element_type=jnp.float32)
    projected = projected.astype(jnp.bfloat16).reshape(clips, TOK, WIDTH)
    return projected, grad_queries, grad_keys, grad_values
```

```python
import jax
import jax.numpy as jnp
from jax import lax
from jax.experimental import pallas as pl
from jax.experimental.pallas import tpu as pltpu
from jax.sharding import PartitionSpec as P

HEAD_DIM = 64
POOL = 4
MEM = 8
SLOT = 112
TILE = 128
F32 = jnp.float32
BF16 = jnp.bfloat16
VMEM_LIMIT = 48 * 1024 * 1024


def dot(a, b):
    return jnp.dot(a, b, preferred_element_type=F32)


def dot_rows(a, b):
    return lax.dot_general(a, b, (((0,), (0,)), ((), ())), preferred_element_type=F32)


def dot_cols(a, b):
    return lax.dot_general(a, b, (((1,), (1,)), ((), ())), preferred_element_type=F32)


def call(body, outs, flops, moved, n_in, scalars=0, scratch=()):
    smem = pl.BlockSpec(memory_space=pltpu.SMEM)
    vmem = pl.BlockSpec(memory_space=pltpu.VMEM)
    return pl.pallas_call(
        body,
        out_shape=tuple(jax.ShapeDtypeStruct(s, d) for s, d in outs),
        in_specs=[smem] * scalars + [vmem] * n_in,
        out_specs=tuple(vmem for _ in outs),
        scratch_shapes=list(scratch),
        compiler_params=pltpu.CompilerParams(vmem_limit_bytes=VMEM_LIMIT),
        cost_estimate=pl.CostEstimate(flops=flops, bytes_accessed=moved, transcendentals=0),
    )


def pool_body(start_ref, k_ref, v_ref, out_ref):
    tokens = k_ref.shape[0]
    pooled = tokens // POOL
    row = lax.broadcasted_iota(jnp.int32, (SLOT, tokens), 0)
    col = lax.broadcasted_iota(jnp.int32, (SLOT, tokens), 1)
    matrix = jnp.where((col >> 2) == row, 1.0 / POOL, 0.0).astype(BF16)
    flag = start_ref[0].astype(F32)
    rows = lax.broadcasted_iota(jnp.int32, (SLOT, TILE), 0)
    out_ref[0] = jnp.where(rows < pooled, dot(matrix, k_ref[...]), flag).astype(BF16)
    out_ref[1] = dot(matrix, v_ref[...]).astype(BF16)


def stacked(x, width):
    tokens = x.shape[0]
    lane = lax.broadcasted_iota(jnp.int32, x.shape, 1)
    low = jnp.where(lane < HEAD_DIM, x, 0.0)
    high = jnp.where(lane < HEAD_DIM, 0.0, x)
    return jnp.concatenate([low, high, jnp.zeros((width - 2 * tokens, TILE), F32)], axis=0)


def unstacked(xt, tokens):
    x = xt.T
    lane = lax.broadcasted_iota(jnp.int32, (tokens, TILE), 1)
    return jnp.where(lane < HEAD_DIM, x[:tokens], x[tokens : 2 * tokens])


def own_body(q_ref, k_ref, v_ref, og_ref, w_ref, qs_ref, qst_ref, dos_ref, dost_ref, m_ref, l_ref, ot_ref):
    width = qs_ref.shape[0]
    q = stacked(q_ref[...].astype(F32) * HEAD_DIM**-0.5, width)
    qs_ref[...] = q.astype(BF16)
    qst = q.T.astype(BF16)
    qst_ref[...] = qst
    grad = dot_cols(og_ref[...], w_ref[...]).astype(BF16).astype(F32)
    grad = stacked(grad, width)
    dos_ref[...] = grad.astype(BF16)
    dost_ref[...] = grad.T.astype(BF16)
    scores = dot(k_ref[...], qst)
    peak = jnp.max(scores, axis=0, keepdims=True)
    expo = jnp.exp(scores - peak)
    m_ref[...] = peak
    l_ref[...] = jnp.sum(expo, axis=0, keepdims=True)
    ot_ref[...] = dot_rows(v_ref[...], expo.astype(BF16))


def memory_body(
    start_ref,
    q_ref, mem_ref, qs_ref, qst_ref, dos_ref, dost_ref, m_ref, l_ref, ot_ref,
    pay_ref, att_ref, mn_ref, inv_ref, delta_ref, dqt_ref,
    s_ref, p_ref, ds_ref, mk_ref, mv_ref,
):
    width = qs_ref.shape[0]
    tiles = width // TILE
    parts, rows_each = att_ref.shape[0], att_ref.shape[1]
    tokens = q_ref.shape[0]
    pooled = tokens // POOL
    position = lax.axis_index("tm")
    place = lax.rem(position, MEM)
    group = lax.div(position, MEM)
    started = [mem_ref[k, 0, pl.ds(96, 16), :].astype(F32)[8:16] for k in range(MEM)]
    ages = [lax.rem(place - k - 1 + 2 * MEM, MEM) for k in range(MEM)]
    own_start = start_ref[0].astype(F32)
    row = lax.broadcasted_iota(jnp.int32, (SLOT, TILE), 0)
    peaks = [None] * tiles
    for k in range(MEM):
        absent = jnp.where((group == 0) & (place <= k), 1.0, 0.0) + own_start
        blocked = jnp.full((8, TILE), absent, F32)
        for other in range(MEM):
            if other != k:
                blocked = blocked + started[other] * jnp.where(ages[other] < ages[k], 1.0, 0.0)
        mk_ref[pl.ds(k * SLOT, SLOT), :] = mem_ref[k, 0]
        mv_ref[pl.ds(k * SLOT, SLOT), :] = mem_ref[k, 1]
        scores = dot(mem_ref[k, 0], qst_ref[...])
        keep = (jnp.concatenate([blocked] * (SLOT // 8), axis=0) == 0.0) & (row < pooled)
        for t in range(tiles):
            piece = jnp.where(keep, scores[:, t * TILE : (t + 1) * TILE], -1e30)
            s_ref[pl.ds(k * SLOT, SLOT), pl.ds(t * TILE, TILE)] = piece
            top = jnp.max(piece.reshape(SLOT // 8, 8, TILE), axis=0)
            peaks[t] = top if peaks[t] is None else jnp.maximum(peaks[t], top)
    for t in range(tiles):
        lanes = pl.ds(t * TILE, TILE)
        own_peak = m_ref[:, lanes]
        peak = jnp.maximum(own_peak, jnp.max(peaks[t], axis=0, keepdims=True))
        total = None
        for k in range(MEM):
            rows = pl.ds(k * SLOT, SLOT)
            expo = jnp.exp(s_ref[rows, lanes] - peak)
            s_ref[rows, lanes] = expo
            part = jnp.sum(expo.reshape(SLOT // 8, 8, TILE), axis=0)
            total = part if total is None else total + part
        factor = jnp.exp(own_peak - peak)
        inverse = 1.0 / (jnp.sum(total, axis=0, keepdims=True) + l_ref[:, lanes] * factor)
        mn_ref[:, lanes] = peak
        inv_ref[:, lanes] = inverse
        for k in range(MEM):
            rows = pl.ds(k * SLOT, SLOT)
            probs = s_ref[rows, lanes] * inverse
            s_ref[rows, lanes] = probs
            p_ref[rows, lanes] = probs.astype(BF16)
        ot_ref_piece = ot_ref[:, lanes] * (factor * inverse)
        dqt_ref[:, lanes] = ot_ref_piece
    out_t = dqt_ref[...] + dot_rows(mv_ref[...], p_ref[...])
    delta = jnp.sum(out_t * dost_ref[...].astype(F32), axis=0, keepdims=True)
    delta_ref[...] = delta
    attended = unstacked(out_t, tokens)
    each = tokens // parts
    for part in range(parts):
        piece = attended[part * each : (part + 1) * each]
        piece = jnp.concatenate([piece, jnp.zeros((rows_each - each, TILE), F32)], axis=0)
        att_ref[part] = piece.astype(BF16)
    for k in range(MEM):
        rows = pl.ds(k * SLOT, SLOT)
        grad_probs = dot(mem_ref[k, 1], dost_ref[...])
        for t in range(tiles):
            lanes = pl.ds(t * TILE, TILE)
            piece = s_ref[rows, lanes] * (grad_probs[:, t * TILE : (t + 1) * TILE] - delta_ref[:, lanes])
            ds_ref[rows, lanes] = piece.astype(BF16)
        pay_ref[k, 0] = dot(ds_ref[rows, :], qs_ref[...]).astype(BF16)
        pay_ref[k, 1] = dot(p_ref[rows, :], dos_ref[...]).astype(BF16)
    dqt_ref[...] = dot_rows(mk_ref[...], ds_ref[...])


def back_body(
    k_ref, v_ref, qs_ref, qst_ref, dos_ref, dost_ref, m_ref, inv_ref, delta_ref, dqt_ref,
    gq_ref, own_ref,
):
    tokens = k_ref.shape[0]
    scores = dot(k_ref[...], qst_ref[...])
    probs = jnp.exp(scores - m_ref[...]) * inv_ref[...]
    grad_probs = dot(v_ref[...], dost_ref[...])
    grad_scores = (probs * (grad_probs - delta_ref[...])).astype(BF16)
    own_ref[0] = dot(grad_scores, qs_ref[...])
    own_ref[1] = dot(probs.astype(BF16), dos_ref[...])
    grad_t = (dqt_ref[...] + dot_rows(k_ref[...], grad_scores)) * HEAD_DIM**-0.5
    gq_ref[...] = unstacked(grad_t, tokens).astype(BF16)


def sum_body(got_ref, prev_ref, own_ref):
    place = lax.rem(lax.axis_index("tm"), MEM)
    prev = jnp.zeros(own_ref.shape, F32)
    own = jnp.zeros(own_ref.shape, F32)
    for i in range(MEM):
        block = got_ref[i].astype(F32)
        share = jnp.where(i <= place, 1.0, 0.0)
        prev = prev + block * share
        own = own + block * (1.0 - share)
    prev_ref[...] = prev.astype(BF16)
    own_ref[...] = own


def final_body(direct_ref, near_ref, far_ref, gk_ref, gv_ref):
    tokens = gk_ref.shape[0]
    row = lax.broadcasted_iota(jnp.int32, (tokens, SLOT), 0)
    col = lax.broadcasted_iota(jnp.int32, (tokens, SLOT), 1)
    matrix = jnp.where((row >> 2) == col, 1.0 / POOL, 0.0).astype(BF16)
    for which, out_ref in enumerate((gk_ref, gv_ref)):
        total = near_ref[which] + far_ref[which].astype(F32)
        high = total.astype(BF16)
        low = (total - high.astype(F32)).astype(BF16)
        spread = dot(matrix, high) + dot(matrix, low)
        out_ref[...] = (direct_ref[which] + spread).astype(BF16)


def project_body(att_ref, w_ref, mine_ref, other_ref):
    odd = lax.rem(lax.axis_index("head"), 2)
    parts = att_ref.shape[0]
    rows = mine_ref.shape[0]
    total = dot(att_ref[0], w_ref[0])
    for part in range(1, parts):
        total = total + dot(att_ref[part], w_ref[part])
    first, second = total[:rows], total[rows : 2 * rows]
    take = jnp.full(first.shape, odd, jnp.int32) == 1
    mine_ref[...] = jnp.where(take, second, first)
    other_ref[...] = jnp.where(take, first, second).astype(BF16)


def local(queries, key_tokens, value_tokens, out_weight, out_grad, clip_starts):
    q, k, v, grad = queries[0], key_tokens[0], value_tokens[0], out_grad[0]
    tokens = q.shape[0]
    clips = lax.axis_size("tm")
    heads = lax.axis_size("head")
    model = out_weight.shape[1]
    width = 7 * TILE
    groups = [list(range(s, s + MEM)) for s in range(0, clips, MEM)]
    sides = [list(range(s, heads, 2)) for s in range(2)]
    parts = heads // 2
    each = tokens // parts
    place = lax.axis_index("tm") % MEM

    weights = lax.all_gather(out_weight, "head", axis_index_groups=sides)

    (own,) = call(pool_body, [((2, SLOT, TILE), BF16)], 10**7, 10**6, 2, 1)(clip_starts, k, v)
    prev = lax.ppermute(own, "tm", [(c, c + MEM) for c in range(clips - MEM)])
    qs, qst, dos, dost, m_own, l_own, ot_own = call(
        own_body,
        [
            ((width, TILE), BF16), ((TILE, width), BF16), ((width, TILE), BF16), ((TILE, width), BF16),
            ((1, width), F32), ((1, width), F32), ((TILE, width), F32),
        ],
        2 * 10**9, 2 * 10**6, 5,
    )(q, k, v, grad, out_weight)
    later = jnp.arange(MEM)[:, None, None, None] > place
    outgoing = jnp.where(later, own[None], prev[None])
    memory = lax.all_to_all(outgoing, "tm", 0, 0, axis_index_groups=groups)
    payload, attended, m_all, inverse, delta, dqt = call(
        memory_body,
        [
            ((MEM, 2, SLOT, TILE), BF16), ((parts, SLOT, TILE), BF16),
            ((1, width), F32), ((1, width), F32), ((1, width), F32), ((TILE, width), F32),
        ],
        4 * 10**9, 4 * 10**6, 9, 1,
        [
            pltpu.VMEM((MEM * SLOT, width), F32), pltpu.VMEM((MEM * SLOT, width), BF16),
            pltpu.VMEM((MEM * SLOT, width), BF16), pltpu.VMEM((MEM * SLOT, TILE), BF16),
            pltpu.VMEM((MEM * SLOT, TILE), BF16),
        ],
    )(clip_starts, q, memory, qs, qst, dos, dost, m_own, l_own, ot_own)
    arrived = lax.all_to_all(payload, "tm", 0, 0, axis_index_groups=groups)
    rows_of_all = lax.all_to_all(attended, "head", 0, 0, axis_index_groups=sides)
    gq, direct = call(
        back_body, [((tokens, TILE), BF16), ((2, tokens, TILE), F32)], 2 * 10**9, 2 * 10**6, 10
    )(k, v, qs, qst, dos, dost, m_all, inverse, delta, dqt)
    back, near = call(
        sum_body, [((2, SLOT, TILE), BF16), ((2, SLOT, TILE), F32)], 10**6, 10**6, 1
    )(arrived)
    far = lax.ppermute(back, "tm", [(c + MEM, c) for c in range(clips - MEM)])
    mine, other = call(
        project_body, [((each // 2, model), F32), ((each // 2, model), BF16)], 10**9, 2 * 10**6, 2
    )(rows_of_all, weights)
    theirs = lax.ppermute(other, "head", [(h, h ^ 1) for h in range(heads)])
    projected = (mine + theirs.astype(F32)).astype(BF16)
    gk, gv = call(
        final_body, [((tokens, TILE), BF16), ((tokens, TILE), BF16)], 10**7, 10**6, 3
    )(direct, near, far)
    return projected[None], gq[None], gk[None], gv[None]


def solution(mesh):
    return jax.shard_map(
        local,
        mesh=mesh,
        in_specs=(
            P("tm", None, "head"),
            P("tm", None, "head"),
            P("tm", None, "head"),
            P("head", None),
            P("tm", None, None),
            P("tm"),
        ),
        out_specs=(
            P("tm", "head", None),
            P("tm", None, "head"),
            P("tm", None, "head"),
            P("tm", None, "head"),
        ),
        check_vma=False,
    )
```

```python
import jax
import jax.numpy as jnp
from jax import lax
from jax.experimental import pallas as pl
from jax.experimental.pallas import tpu as pltpu
from jax.sharding import PartitionSpec as P

HEAD_DIM = 64
POOL = 4
MEM = 8
SLOT = 112
TILE = 128
F32 = jnp.float32
BF16 = jnp.bfloat16
VMEM_LIMIT = 20 * 1024 * 1024


def dot(a, b):
    return jnp.dot(a, b, preferred_element_type=F32)


def dot_rows(a, b):
    return lax.dot_general(a, b, (((0,), (0,)), ((), ())), preferred_element_type=F32)


def dot_cols(a, b):
    return lax.dot_general(a, b, (((1,), (1,)), ((), ())), preferred_element_type=F32)


def call(body, outs, flops, moved, n_in, scalars=0, scratch=(), spaces=None, limit=VMEM_LIMIT):
    smem = pl.BlockSpec(memory_space=pltpu.SMEM)
    vmem = pl.BlockSpec(memory_space=pltpu.VMEM)
    return pl.pallas_call(
        body,
        out_shape=tuple(jax.ShapeDtypeStruct(s, d) for s, d in outs),
        in_specs=[smem] * scalars + [
            pl.BlockSpec(memory_space=space) for space in spaces or [pltpu.VMEM] * n_in
        ],
        out_specs=tuple(vmem for _ in outs),
        scratch_shapes=list(scratch),
        compiler_params=pltpu.CompilerParams(vmem_limit_bytes=limit),
        cost_estimate=pl.CostEstimate(flops=flops, bytes_accessed=moved, transcendentals=0),
    )


def pool_body(start_ref, k_hbm, v_hbm, out_ref, k_ref, v_ref, sems):
    loads = [
        pltpu.make_async_copy(k_hbm, k_ref, sems.at[0]),
        pltpu.make_async_copy(v_hbm, v_ref, sems.at[1]),
    ]
    for load in loads:
        load.start()
    tokens = k_ref.shape[0]
    pooled = tokens // POOL
    row = lax.broadcasted_iota(jnp.int32, (SLOT, tokens), 0)
    col = lax.broadcasted_iota(jnp.int32, (SLOT, tokens), 1)
    matrix = jnp.where((col >> 2) == row, 1.0 / POOL, 0.0).astype(BF16)
    flag = start_ref[0].astype(F32)
    for load in loads:
        load.wait()
    rows = lax.broadcasted_iota(jnp.int32, (SLOT, TILE), 0)
    out_ref[0] = jnp.where(rows < pooled, dot(matrix, k_ref[...]), flag).astype(BF16)
    out_ref[1] = dot(matrix, v_ref[...]).astype(BF16)


def choose_body(own_ref, prev_ref, out_ref):
    place = lax.rem(lax.axis_index("tm"), MEM)
    own = own_ref[...].astype(F32)
    prev = prev_ref[...].astype(F32)
    for k in range(MEM):
        ours = jnp.full(own.shape, place, jnp.int32) < k
        out_ref[k] = jnp.where(ours, own, prev).astype(BF16)


def stacked(x, width):
    tokens = x.shape[0]
    lane = lax.broadcasted_iota(jnp.int32, x.shape, 1)
    low = jnp.where(lane < HEAD_DIM, x, 0.0)
    high = jnp.where(lane < HEAD_DIM, 0.0, x)
    return jnp.concatenate([low, high, jnp.zeros((width - 2 * tokens, TILE), F32)], axis=0)


def unstacked(xt, tokens):
    x = xt.T
    lane = lax.broadcasted_iota(jnp.int32, (tokens, TILE), 1)
    return jnp.where(lane < HEAD_DIM, x[:tokens], x[tokens : 2 * tokens])


def prepare_body(og_ref, w_ref, grad_ref, dost_ref):
    width = dost_ref.shape[1]
    grad = dot_cols(og_ref[...], w_ref[...]).astype(BF16)
    grad_ref[...] = grad
    dost_ref[...] = stacked(grad.astype(F32), width).T.astype(BF16)


def own_body(q_ref, k_ref, v_ref, m_ref, l_ref, ot_ref):
    width = ot_ref.shape[1]
    qs = stacked(q_ref[...].astype(F32) * HEAD_DIM**-0.5, width).astype(BF16)
    scores = dot_cols(k_ref[...], qs)
    peak = jnp.max(scores, axis=0, keepdims=True)
    expo = jnp.exp(scores - peak)
    m_ref[...] = peak
    l_ref[...] = jnp.sum(expo, axis=0, keepdims=True)
    ot_ref[...] = dot_rows(v_ref[...], expo.astype(BF16))


def memory_body(
    start_ref,
    q_ref, grad_ref, mem_ref, m_ref, l_ref, dost_hbm, ot_hbm,
    pay_ref, keep_ref, give_ref, mn_ref, inv_ref, delta_ref, dqt_ref,
    s_ref, p_ref, ds_ref, mk_ref, mv_ref, qs_ref, dos_ref, dost_ref, ot_ref, sems,
):
    width = qs_ref.shape[0]
    loads = [
        pltpu.make_async_copy(dost_hbm, dost_ref, sems.at[0]),
        pltpu.make_async_copy(ot_hbm, ot_ref, sems.at[1]),
    ]
    for load in loads:
        load.start()
    qs_ref[...] = stacked(q_ref[...].astype(F32) * HEAD_DIM**-0.5, width).astype(BF16)
    dos_ref[...] = stacked(grad_ref[...].astype(F32), width).astype(BF16)
    tiles = width // TILE
    tokens = q_ref.shape[0]
    pooled = tokens // POOL
    position = lax.axis_index("tm")
    place = lax.rem(position, MEM)
    group = lax.div(position, MEM)
    started = [mem_ref[k, 0, pl.ds(96, 16), :].astype(F32)[8:16] for k in range(MEM)]
    ages = [lax.rem(place - k - 1 + 2 * MEM, MEM) for k in range(MEM)]
    own_start = start_ref[0].astype(F32)
    row = lax.broadcasted_iota(jnp.int32, (SLOT, TILE), 0)
    peaks = [None] * tiles
    for k in range(MEM):
        absent = jnp.where((group == 0) & (place <= k), 1.0, 0.0) + own_start
        blocked = jnp.full((8, TILE), absent, F32)
        for other in range(MEM):
            if other != k:
                blocked = blocked + started[other] * jnp.where(ages[other] < ages[k], 1.0, 0.0)
        mk_ref[pl.ds(k * SLOT, SLOT), :] = mem_ref[k, 0]
        mv_ref[pl.ds(k * SLOT, SLOT), :] = mem_ref[k, 1]
        scores = dot_cols(mem_ref[k, 0], qs_ref[...])
        keep = (jnp.concatenate([blocked] * (SLOT // 8), axis=0) == 0.0) & (row < pooled)
        for t in range(tiles):
            piece = jnp.where(keep, scores[:, t * TILE : (t + 1) * TILE], -1e30)
            s_ref[pl.ds(k * SLOT, SLOT), pl.ds(t * TILE, TILE)] = piece
            top = jnp.max(piece.reshape(SLOT // 8, 8, TILE), axis=0)
            peaks[t] = top if peaks[t] is None else jnp.maximum(peaks[t], top)
    for load in loads:
        load.wait()
    for t in range(tiles):
        lanes = pl.ds(t * TILE, TILE)
        own_peak = m_ref[:, lanes]
        peak = jnp.maximum(own_peak, jnp.max(peaks[t], axis=0, keepdims=True))
        total = None
        for k in range(MEM):
            rows = pl.ds(k * SLOT, SLOT)
            expo = jnp.exp(s_ref[rows, lanes] - peak)
            s_ref[rows, lanes] = expo
            part = jnp.sum(expo.reshape(SLOT // 8, 8, TILE), axis=0)
            total = part if total is None else total + part
        factor = jnp.exp(own_peak - peak)
        inverse = 1.0 / (jnp.sum(total, axis=0, keepdims=True) + l_ref[:, lanes] * factor)
        mn_ref[:, lanes] = peak
        inv_ref[:, lanes] = inverse
        for k in range(MEM):
            rows = pl.ds(k * SLOT, SLOT)
            probs = s_ref[rows, lanes] * inverse
            s_ref[rows, lanes] = probs
            p_ref[rows, lanes] = probs.astype(BF16)
        ot_ref_piece = ot_ref[:, lanes] * (factor * inverse)
        dqt_ref[:, lanes] = ot_ref_piece
    out_t = dqt_ref[...] + dot_rows(mv_ref[...], p_ref[...])
    delta = jnp.sum(out_t * dost_ref[...].astype(F32), axis=0, keepdims=True)
    delta_ref[...] = delta
    attended = unstacked(out_t, tokens)
    each = tokens // (4 * keep_ref.shape[0])
    rest = jnp.zeros((keep_ref.shape[1] - 2 * each, TILE), F32)
    pieces = []
    for part in range(2 * keep_ref.shape[0]):
        low = attended[part * each : (part + 1) * each]
        high = attended[(part + 4) * each : (part + 5) * each]
        pieces.append(jnp.concatenate([low, high, rest], axis=0))
    odd = jnp.full(pieces[0].shape, lax.rem(lax.axis_index("head"), 2), jnp.int32) == 1
    for pair in range(keep_ref.shape[0]):
        even_piece, odd_piece = pieces[2 * pair], pieces[2 * pair + 1]
        keep_ref[pair] = jnp.where(odd, odd_piece, even_piece).astype(BF16)
        give_ref[pair] = jnp.where(odd, even_piece, odd_piece).astype(BF16)
    for k in range(MEM):
        rows = pl.ds(k * SLOT, SLOT)
        grad_probs = dot(mem_ref[k, 1], dost_ref[...])
        for t in range(tiles):
            lanes = pl.ds(t * TILE, TILE)
            piece = s_ref[rows, lanes] * (grad_probs[:, t * TILE : (t + 1) * TILE] - delta_ref[:, lanes])
            ds_ref[rows, lanes] = piece.astype(BF16)
        pay_ref[k, 0] = dot(ds_ref[rows, :], qs_ref[...]).astype(BF16)
        pay_ref[k, 1] = dot(p_ref[rows, :], dos_ref[...]).astype(BF16)
    dqt_ref[...] = dot_rows(mk_ref[...], ds_ref[...])


def back_body(
    q_ref, grad_ref, k_ref, v_ref, dost_ref, m_ref, inv_ref, delta_ref, dqt_ref,
    gq_ref, own_ref,
):
    tokens = k_ref.shape[0]
    width = dost_ref.shape[1]
    qs = stacked(q_ref[...].astype(F32) * HEAD_DIM**-0.5, width).astype(BF16)
    dos = stacked(grad_ref[...].astype(F32), width).astype(BF16)
    scores = dot_cols(k_ref[...], qs)
    probs = jnp.exp(scores - m_ref[...]) * inv_ref[...]
    grad_probs = dot(v_ref[...], dost_ref[...])
    grad_scores = (probs * (grad_probs - delta_ref[...])).astype(BF16)
    own_ref[0] = dot(grad_scores, qs)
    own_ref[1] = dot(probs.astype(BF16), dos)
    grad_t = (dqt_ref[...] + dot_rows(k_ref[...], grad_scores)) * HEAD_DIM**-0.5
    gq_ref[...] = unstacked(grad_t, tokens).astype(BF16)


def sum_body(got_ref, prev_ref, own_ref):
    place = lax.rem(lax.axis_index("tm"), MEM)
    prev = jnp.zeros(own_ref.shape, F32)
    own = jnp.zeros(own_ref.shape, F32)
    for i in range(MEM):
        block = got_ref[i].astype(F32)
        share = jnp.where(i <= place, 1.0, 0.0)
        prev = prev + block * share
        own = own + block * (1.0 - share)
    prev_ref[:, :SLOT, :] = prev.astype(BF16)
    prev_ref[:, SLOT:, :] = jnp.zeros((2, TILE - SLOT, TILE), BF16)
    own_ref[...] = own


def final_body(direct_ref, near_ref, far_ref, gk_ref, gv_ref):
    tokens = gk_ref.shape[0]
    row = lax.broadcasted_iota(jnp.int32, (tokens, SLOT), 0)
    col = lax.broadcasted_iota(jnp.int32, (tokens, SLOT), 1)
    matrix = jnp.where((row >> 2) == col, 1.0 / POOL, 0.0).astype(BF16)
    for which, out_ref in enumerate((gk_ref, gv_ref)):
        total = near_ref[which] + far_ref[which].astype(F32)[:SLOT]
        high = total.astype(BF16)
        low = (total - high.astype(F32)).astype(BF16)
        spread = dot(matrix, high) + dot(matrix, low)
        out_ref[...] = (direct_ref[which] + spread).astype(BF16)


def project_body(keep_ref, near_ref, w_ref, chip_ref, mine_ref, other_ref):
    upper = lax.rem(lax.axis_index("head") >> 2, 2)
    core = lax.rem(lax.axis_index("tm"), 2)
    rows = mine_ref.shape[0]
    half = w_ref.shape[1]
    total = None
    for part in range(w_ref.shape[0]):
        att = (keep_ref[part] if part < 2 else near_ref[part - 2]).astype(F32)
        swap = jnp.full(att.shape, core, jnp.int32) == 1
        att = jnp.where(swap, pltpu.roll(att, half, 1), att).astype(BF16)
        term = dot(att[:, :half], w_ref[part]) + dot(att[:, half:], chip_ref[part])
        total = term if total is None else total + term
    first, second = total[:rows], total[rows : 2 * rows]
    take = jnp.full(first.shape, upper, jnp.int32) == 1
    mine_ref[...] = jnp.where(take, second, first)
    other_ref[...] = jnp.where(take, first, second).astype(BF16)


def local(queries, key_tokens, value_tokens, out_weight, out_grad, clip_starts):
    q, k, v, grad = queries[0], key_tokens[0], value_tokens[0], out_grad[0]
    tokens = q.shape[0]
    clips = lax.axis_size("tm")
    heads = lax.axis_size("head")
    model = out_weight.shape[1]
    width = 7 * TILE
    groups = [list(range(s, s + MEM)) for s in range(0, clips, MEM)]
    me = lax.axis_index("head")
    core = lax.axis_index("tm") % 2
    half = out_weight.shape[0] // 2
    w_half = lax.dynamic_slice_in_dim(out_weight, core * half, half, 0)
    by_one, by_two, by_four = ([(h, h ^ step) for h in range(heads)] for step in (1, 2, 4))

    (own,) = call(
        pool_body, [((2, SLOT, TILE), BF16)], 10**7, 10**6, 2, 1,
        [pltpu.VMEM(k.shape, BF16), pltpu.VMEM(v.shape, BF16), pltpu.SemaphoreType.DMA((2,))],
        [pltpu.HBM] * 2, 60 * 1024 * 1024,
    )(clip_starts, k, v)
    prev = lax.ppermute(own, "tm", [(c, c + MEM) for c in range(clips - MEM)])
    grad, _ = lax.optimization_barrier((grad, own))
    grad_rows, dost = call(
        prepare_body, [((tokens, TILE), BF16), ((TILE, width), BF16)], 10**9, 2 * 10**6, 2
    )(grad, out_weight)
    w_one = lax.ppermute(w_half, "head", by_one)
    prev, grad_rows, w_one = lax.optimization_barrier((prev, grad_rows, w_one))
    w_pair = jnp.stack([w_half, w_one])
    (outgoing,) = call(choose_body, [((MEM, 2, SLOT, TILE), BF16)], 10**6, 10**6, 2)(own, prev)
    memory = lax.all_to_all(outgoing, "tm", 0, 0, axis_index_groups=groups)
    q_now, _ = lax.optimization_barrier((q, outgoing))
    m_own, l_own, ot_own = call(
        own_body, [((1, width), F32), ((1, width), F32), ((TILE, width), F32)], 10**9, 10**6, 3
    )(q_now, k, v)
    w_sent, m_own = lax.optimization_barrier((w_pair, m_own))
    w_two = lax.ppermute(w_sent, "head", by_two)
    payload, a_keep, a_give, m_all, inverse, delta, dqt = call(
        memory_body,
        [
            ((MEM, 2, SLOT, TILE), BF16), ((2, SLOT, TILE), BF16), ((2, SLOT, TILE), BF16),
            ((1, width), F32), ((1, width), F32), ((1, width), F32), ((TILE, width), F32),
        ],
        4 * 10**9, 4 * 10**6, 7, 1,
        [
            pltpu.VMEM((MEM * SLOT, width), F32), pltpu.VMEM((MEM * SLOT, width), BF16),
            pltpu.VMEM((MEM * SLOT, width), BF16), pltpu.VMEM((MEM * SLOT, TILE), BF16),
            pltpu.VMEM((MEM * SLOT, TILE), BF16), pltpu.VMEM((width, TILE), BF16),
            pltpu.VMEM((width, TILE), BF16), pltpu.VMEM((TILE, width), BF16),
            pltpu.VMEM((TILE, width), F32), pltpu.SemaphoreType.DMA((2,)),
        ],
        [pltpu.VMEM] * 5 + [pltpu.HBM] * 2,
    )(clip_starts, q, grad_rows, memory, m_own, l_own, dost, ot_own)
    arrived = lax.all_to_all(payload, "tm", 0, 0, axis_index_groups=groups)
    a_one = lax.ppermute(a_give, "head", by_one)
    w_pair, w_two, _ = lax.optimization_barrier((w_pair, w_two, a_keep))
    w_four = jnp.concatenate([w_pair, w_two])
    w_chip = lax.ppermute(w_four, "tm", [(c, c ^ 1) for c in range(clips)])
    back, near = call(
        sum_body, [((2, TILE, TILE), BF16), ((2, SLOT, TILE), F32)], 10**6, 10**6, 1
    )(arrived)
    far = lax.ppermute(back, "tm", [(c + MEM, c) for c in range(clips - MEM)])
    dost_now, _ = lax.optimization_barrier((dost, back))
    gq, direct = call(
        back_body, [((tokens, TILE), BF16), ((2, tokens, TILE), F32)], 2 * 10**9, 2 * 10**6, 9
    )(q, grad_rows, k, v, dost_now, m_all, inverse, delta, dqt)
    low = (me >> 1) & 1
    a_pair = jnp.stack([a_keep, a_one])
    a_stay = lax.dynamic_slice_in_dim(a_pair, low, 1, 1)[:, 0]
    a_send = lax.dynamic_slice_in_dim(a_pair, 1 - low, 1, 1)[:, 0]
    a_two = lax.ppermute(a_send, "head", by_two)
    a_two, _ = lax.optimization_barrier((a_two, back))
    mine, other = call(
        project_body, [((tokens // heads, model), F32), ((tokens // heads, model), BF16)], 10**4, 10**4, 4
    )(a_stay, a_two, w_four, w_chip)
    theirs = lax.ppermute(other, "head", by_four)
    projected = (mine + theirs.astype(F32)).astype(BF16)
    gk, gv = call(
        final_body, [((tokens, TILE), BF16), ((tokens, TILE), BF16)], 4 * 10**10, 10**6, 3
    )(direct, near, far)
    return projected[None], gq[None], gk[None], gv[None]


def solution(mesh):
    return jax.shard_map(
        local,
        mesh=mesh,
        in_specs=(
            P("tm", None, "head"),
            P("tm", None, "head"),
            P("tm", None, "head"),
            P("head", None),
            P("tm", None, None),
            P("tm"),
        ),
        out_specs=(
            P("tm", "head", None),
            P("tm", None, "head"),
            P("tm", None, "head"),
            P("tm", None, "head"),
        ),
        check_vma=False,
    )
```

```python
import jax
import jax.numpy as jnp
from jax import lax
from jax.experimental import pallas as pl
from jax.experimental.pallas import tpu as pltpu
from jax.sharding import PartitionSpec as P

HEAD_DIM = 64
POOL = 4
MEM = 8
SLOT = 112
TILE = 128
F32 = jnp.float32
BF16 = jnp.bfloat16
VMEM_LIMIT = 20 * 1024 * 1024


def dot(a, b):
    return jnp.dot(a, b, preferred_element_type=F32)


def dot_rows(a, b):
    return lax.dot_general(a, b, (((0,), (0,)), ((), ())), preferred_element_type=F32)


def dot_cols(a, b):
    return lax.dot_general(a, b, (((1,), (1,)), ((), ())), preferred_element_type=F32)


def call(body, outs, flops, moved, n_in, scalars=0, scratch=(), spaces=None, limit=VMEM_LIMIT):
    smem = pl.BlockSpec(memory_space=pltpu.SMEM)
    vmem = pl.BlockSpec(memory_space=pltpu.VMEM)
    return pl.pallas_call(
        body,
        out_shape=tuple(jax.ShapeDtypeStruct(s, d) for s, d in outs),
        in_specs=[smem] * scalars + [
            pl.BlockSpec(memory_space=space) for space in spaces or [pltpu.VMEM] * n_in
        ],
        out_specs=tuple(vmem for _ in outs),
        scratch_shapes=list(scratch),
        compiler_params=pltpu.CompilerParams(vmem_limit_bytes=limit),
        cost_estimate=pl.CostEstimate(flops=flops, bytes_accessed=moved, transcendentals=0),
    )


def pool_body(start_ref, k_hbm, v_hbm, out_ref, k_ref, v_ref, sems):
    loads = [
        pltpu.make_async_copy(k_hbm, k_ref, sems.at[0]),
        pltpu.make_async_copy(v_hbm, v_ref, sems.at[1]),
    ]
    for load in loads:
        load.start()
    tokens = k_ref.shape[0]
    pooled = tokens // POOL
    row = lax.broadcasted_iota(jnp.int32, (SLOT, tokens), 0)
    col = lax.broadcasted_iota(jnp.int32, (SLOT, tokens), 1)
    matrix = jnp.where((col >> 2) == row, 1.0 / POOL, 0.0).astype(BF16)
    flag = start_ref[0].astype(F32)
    for load in loads:
        load.wait()
    rows = lax.broadcasted_iota(jnp.int32, (SLOT, TILE), 0)
    out_ref[0] = jnp.where(rows < pooled, dot(matrix, k_ref[...]), flag).astype(BF16)
    out_ref[1] = dot(matrix, v_ref[...]).astype(BF16)


def choose_body(own_ref, prev_ref, out_ref):
    place = lax.rem(lax.axis_index("tm"), MEM)
    own = own_ref[...].astype(F32)
    prev = prev_ref[...].astype(F32)
    for k in range(MEM):
        ours = jnp.full(own.shape, place, jnp.int32) < k
        out_ref[k] = jnp.where(ours, own, prev).astype(BF16)


def stacked(x, width):
    tokens = x.shape[0]
    lane = lax.broadcasted_iota(jnp.int32, x.shape, 1)
    low = jnp.where(lane < HEAD_DIM, x, 0.0)
    high = jnp.where(lane < HEAD_DIM, 0.0, x)
    return jnp.concatenate([low, high, jnp.zeros((width - 2 * tokens, TILE), F32)], axis=0)


def unstacked(xt, tokens):
    x = xt.T
    lane = lax.broadcasted_iota(jnp.int32, (tokens, TILE), 1)
    return jnp.where(lane < HEAD_DIM, x[:tokens], x[tokens : 2 * tokens])


def prepare_body(og_ref, w_ref, grad_ref, dost_ref):
    width = dost_ref.shape[1]
    grad = dot_cols(og_ref[...], w_ref[...]).astype(BF16)
    grad_ref[...] = grad
    dost_ref[...] = stacked(grad.astype(F32), width).T.astype(BF16)


def own_body(q_ref, k_ref, v_ref, m_ref, l_ref, ot_ref):
    width = ot_ref.shape[1]
    qs = stacked(q_ref[...].astype(F32) * HEAD_DIM**-0.5, width).astype(BF16)
    scores = dot_cols(k_ref[...], qs)
    peak = jnp.max(scores, axis=0, keepdims=True)
    expo = jnp.exp(scores - peak)
    m_ref[...] = peak
    l_ref[...] = jnp.sum(expo, axis=0, keepdims=True)
    ot_ref[...] = dot_rows(v_ref[...], expo.astype(BF16))


def memory_body(
    start_ref,
    q_ref, grad_ref, mem_ref, m_ref, l_ref, dost_hbm, ot_hbm,
    pay_ref, keep_ref, give_ref, mn_ref, inv_ref, delta_ref, dqt_ref,
    s_ref, p_ref, ds_ref, mk_ref, mv_ref, qs_ref, dos_ref, dost_ref, ot_ref, sems,
):
    width = qs_ref.shape[0]
    loads = [
        pltpu.make_async_copy(dost_hbm, dost_ref, sems.at[0]),
        pltpu.make_async_copy(ot_hbm, ot_ref, sems.at[1]),
    ]
    for load in loads:
        load.start()
    qs_ref[...] = stacked(q_ref[...].astype(F32) * HEAD_DIM**-0.5, width).astype(BF16)
    dos_ref[...] = stacked(grad_ref[...].astype(F32), width).astype(BF16)
    tiles = width // TILE
    tokens = q_ref.shape[0]
    pooled = tokens // POOL
    position = lax.axis_index("tm")
    place = lax.rem(position, MEM)
    group = lax.div(position, MEM)
    started = [mem_ref[k, 0, pl.ds(96, 16), :].astype(F32)[8:16] for k in range(MEM)]
    ages = [lax.rem(place - k - 1 + 2 * MEM, MEM) for k in range(MEM)]
    own_start = start_ref[0].astype(F32)
    row = lax.broadcasted_iota(jnp.int32, (SLOT, TILE), 0)
    peaks = [None] * tiles
    for k in range(MEM):
        absent = jnp.where((group == 0) & (place <= k), 1.0, 0.0) + own_start
        blocked = jnp.full((8, TILE), absent, F32)
        for other in range(MEM):
            if other != k:
                blocked = blocked + started[other] * jnp.where(ages[other] < ages[k], 1.0, 0.0)
        mk_ref[pl.ds(k * SLOT, SLOT), :] = mem_ref[k, 0]
        mv_ref[pl.ds(k * SLOT, SLOT), :] = mem_ref[k, 1]
        scores = dot_cols(mem_ref[k, 0], qs_ref[...])
        keep = (jnp.concatenate([blocked] * (SLOT // 8), axis=0) == 0.0) & (row < pooled)
        for t in range(tiles):
            piece = jnp.where(keep, scores[:, t * TILE : (t + 1) * TILE], -1e30)
            s_ref[pl.ds(k * SLOT, SLOT), pl.ds(t * TILE, TILE)] = piece
            top = jnp.max(piece.reshape(SLOT // 8, 8, TILE), axis=0)
            peaks[t] = top if peaks[t] is None else jnp.maximum(peaks[t], top)
    for load in loads:
        load.wait()
    for t in range(tiles):
        lanes = pl.ds(t * TILE, TILE)
        own_peak = m_ref[:, lanes]
        peak = jnp.maximum(own_peak, jnp.max(peaks[t], axis=0, keepdims=True))
        total = None
        for k in range(MEM):
            rows = pl.ds(k * SLOT, SLOT)
            expo = jnp.exp(s_ref[rows, lanes] - peak)
            s_ref[rows, lanes] = expo
            part = jnp.sum(expo.reshape(SLOT // 8, 8, TILE), axis=0)
            total = part if total is None else total + part
        factor = jnp.exp(own_peak - peak)
        inverse = 1.0 / (jnp.sum(total, axis=0, keepdims=True) + l_ref[:, lanes] * factor)
        mn_ref[:, lanes] = peak
        inv_ref[:, lanes] = inverse
        for k in range(MEM):
            rows = pl.ds(k * SLOT, SLOT)
            probs = s_ref[rows, lanes] * inverse
            s_ref[rows, lanes] = probs
            p_ref[rows, lanes] = probs.astype(BF16)
        ot_ref_piece = ot_ref[:, lanes] * (factor * inverse)
        dqt_ref[:, lanes] = ot_ref_piece
    out_t = dqt_ref[...] + dot_rows(mv_ref[...], p_ref[...])
    delta = jnp.sum(out_t * dost_ref[...].astype(F32), axis=0, keepdims=True)
    delta_ref[...] = delta
    attended = unstacked(out_t, tokens)
    each = tokens // (4 * keep_ref.shape[0])
    rest = jnp.zeros((keep_ref.shape[1] - 2 * each, TILE), F32)
    pieces = []
    for part in range(2 * keep_ref.shape[0]):
        low = attended[part * each : (part + 1) * each]
        high = attended[(part + 4) * each : (part + 5) * each]
        pieces.append(jnp.concatenate([low, high, rest], axis=0))
    odd = jnp.full(pieces[0].shape, lax.rem(lax.axis_index("head"), 2), jnp.int32) == 1
    for pair in range(keep_ref.shape[0]):
        even_piece, odd_piece = pieces[2 * pair], pieces[2 * pair + 1]
        keep_ref[pair] = jnp.where(odd, odd_piece, even_piece).astype(BF16)
        give_ref[pair] = jnp.where(odd, even_piece, odd_piece).astype(BF16)
    for k in range(MEM):
        rows = pl.ds(k * SLOT, SLOT)
        grad_probs = dot(mem_ref[k, 1], dost_ref[...])
        for t in range(tiles):
            lanes = pl.ds(t * TILE, TILE)
            piece = s_ref[rows, lanes] * (grad_probs[:, t * TILE : (t + 1) * TILE] - delta_ref[:, lanes])
            ds_ref[rows, lanes] = piece.astype(BF16)
        pay_ref[k, 0] = dot(ds_ref[rows, :], qs_ref[...]).astype(BF16)
        pay_ref[k, 1] = dot(p_ref[rows, :], dos_ref[...]).astype(BF16)
    dqt_ref[...] = dot_rows(mk_ref[...], ds_ref[...])


def back_body(
    q_ref, grad_ref, k_ref, v_ref, dost_ref, m_ref, inv_ref, delta_ref, dqt_ref,
    gq_ref, own_ref,
):
    tokens = k_ref.shape[0]
    width = dost_ref.shape[1]
    qs = stacked(q_ref[...].astype(F32) * HEAD_DIM**-0.5, width).astype(BF16)
    dos = stacked(grad_ref[...].astype(F32), width).astype(BF16)
    scores = dot_cols(k_ref[...], qs)
    probs = jnp.exp(scores - m_ref[...]) * inv_ref[...]
    grad_probs = dot(v_ref[...], dost_ref[...])
    grad_scores = (probs * (grad_probs - delta_ref[...])).astype(BF16)
    own_ref[0] = dot(grad_scores, qs)
    own_ref[1] = dot(probs.astype(BF16), dos)
    grad_t = (dqt_ref[...] + dot_rows(k_ref[...], grad_scores)) * HEAD_DIM**-0.5
    gq_ref[...] = unstacked(grad_t, tokens).astype(BF16)


def sum_body(got_ref, prev_ref, own_ref):
    place = lax.rem(lax.axis_index("tm"), MEM)
    prev = jnp.zeros(own_ref.shape, F32)
    own = jnp.zeros(own_ref.shape, F32)
    for i in range(MEM):
        block = got_ref[i].astype(F32)
        share = jnp.where(i <= place, 1.0, 0.0)
        prev = prev + block * share
        own = own + block * (1.0 - share)
    prev_ref[:, :SLOT, :] = prev.astype(BF16)
    prev_ref[:, SLOT:, :] = jnp.zeros((2, TILE - SLOT, TILE), BF16)
    own_ref[...] = own


def final_body(direct_ref, near_ref, far_ref, gk_ref, gv_ref):
    tokens = gk_ref.shape[0]
    row = lax.broadcasted_iota(jnp.int32, (tokens, SLOT), 0)
    col = lax.broadcasted_iota(jnp.int32, (tokens, SLOT), 1)
    matrix = jnp.where((row >> 2) == col, 1.0 / POOL, 0.0).astype(BF16)
    for which, out_ref in enumerate((gk_ref, gv_ref)):
        total = near_ref[which] + far_ref[which].astype(F32)[:SLOT]
        high = total.astype(BF16)
        low = (total - high.astype(F32)).astype(BF16)
        spread = dot(matrix, high) + dot(matrix, low)
        out_ref[...] = (direct_ref[which] + spread).astype(BF16)


def project_body(keep_ref, near_ref, w_ref, chip_ref, mine_ref, other_ref):
    upper = lax.rem(lax.axis_index("head") >> 2, 2)
    core = lax.rem(lax.axis_index("tm"), 2)
    rows = mine_ref.shape[0]
    half = w_ref.shape[1]
    total = None
    for part in range(w_ref.shape[0]):
        att = (keep_ref[part] if part < 2 else near_ref[part - 2]).astype(F32)
        swap = jnp.full(att.shape, core, jnp.int32) == 1
        att = jnp.where(swap, pltpu.roll(att, half, 1), att).astype(BF16)
        term = dot(att[:, :half], w_ref[part]) + dot(att[:, half:], chip_ref[part])
        total = term if total is None else total + term
    first, second = total[:rows], total[rows : 2 * rows]
    take = jnp.full(first.shape, upper, jnp.int32) == 1
    mine_ref[...] = jnp.where(take, second, first)
    other_ref[...] = jnp.where(take, first, second).astype(BF16)


def local(queries, key_tokens, value_tokens, out_weight, out_grad, clip_starts):
    q, k, v, grad = queries[0], key_tokens[0], value_tokens[0], out_grad[0]
    tokens = q.shape[0]
    clips = lax.axis_size("tm")
    heads = lax.axis_size("head")
    model = out_weight.shape[1]
    width = 7 * TILE
    groups = [list(range(s, s + MEM)) for s in range(0, clips, MEM)]
    me = lax.axis_index("head")
    core = lax.axis_index("tm") % 2
    half = out_weight.shape[0] // 2
    by_one, by_two, by_four = ([(h, h ^ step) for h in range(heads)] for step in (1, 2, 4))

    (own,) = call(
        pool_body, [((2, SLOT, TILE), BF16)], 10**7, 10**6, 2, 1,
        [pltpu.VMEM(k.shape, BF16), pltpu.VMEM(v.shape, BF16), pltpu.SemaphoreType.DMA((2,))],
        [pltpu.HBM] * 2, 60 * 1024 * 1024,
    )(clip_starts, k, v)
    prev = lax.ppermute(own, "tm", [(c, c + MEM) for c in range(clips - MEM)])
    grad, _ = lax.optimization_barrier((grad, own))
    grad_rows, dost = call(
        prepare_body, [((tokens, TILE), BF16), ((TILE, width), BF16)], 10**9, 2 * 10**6, 2
    )(grad, out_weight)
    w_seen, _ = lax.optimization_barrier((out_weight, own))
    w_half = lax.dynamic_slice_in_dim(w_seen, core * half, half, 0)
    w_one = lax.ppermute(w_half, "head", by_one)
    prev, grad_rows = lax.optimization_barrier((prev, grad_rows))
    (outgoing,) = call(choose_body, [((MEM, 2, SLOT, TILE), BF16)], 2 * 10**10, 10**6, 2)(own, prev)
    outgoing, w_one = lax.optimization_barrier((outgoing, w_one))
    w_pair = jnp.stack([w_half, w_one])
    memory = lax.all_to_all(outgoing, "tm", 0, 0, axis_index_groups=groups)
    q_now, _ = lax.optimization_barrier((q, outgoing))
    m_own, l_own, ot_own = call(
        own_body, [((1, width), F32), ((1, width), F32), ((TILE, width), F32)], 10**9, 10**6, 3
    )(q_now, k, v)
    w_sent, m_own = lax.optimization_barrier((w_pair, m_own))
    w_two = lax.ppermute(w_sent, "head", by_two)
    payload, a_keep, a_give, m_all, inverse, delta, dqt = call(
        memory_body,
        [
            ((MEM, 2, SLOT, TILE), BF16), ((2, SLOT, TILE), BF16), ((2, SLOT, TILE), BF16),
            ((1, width), F32), ((1, width), F32), ((1, width), F32), ((TILE, width), F32),
        ],
        4 * 10**9, 4 * 10**6, 7, 1,
        [
            pltpu.VMEM((MEM * SLOT, width), F32), pltpu.VMEM((MEM * SLOT, width), BF16),
            pltpu.VMEM((MEM * SLOT, width), BF16), pltpu.VMEM((MEM * SLOT, TILE), BF16),
            pltpu.VMEM((MEM * SLOT, TILE), BF16), pltpu.VMEM((width, TILE), BF16),
            pltpu.VMEM((width, TILE), BF16), pltpu.VMEM((TILE, width), BF16),
            pltpu.VMEM((TILE, width), F32), pltpu.SemaphoreType.DMA((2,)),
        ],
        [pltpu.VMEM] * 5 + [pltpu.HBM] * 2,
    )(clip_starts, q, grad_rows, memory, m_own, l_own, dost, ot_own)
    arrived = lax.all_to_all(payload, "tm", 0, 0, axis_index_groups=groups)
    a_one = lax.ppermute(a_give, "head", by_one)
    w_pair, w_two, _ = lax.optimization_barrier((w_pair, w_two, a_keep))
    w_four = jnp.concatenate([w_pair, w_two])
    w_chip = lax.ppermute(w_four, "tm", [(c, c ^ 1) for c in range(clips)])
    back, near = call(
        sum_body, [((2, TILE, TILE), BF16), ((2, SLOT, TILE), F32)], 2 * 10**10, 10**6, 1
    )(arrived)
    dost_now, _ = lax.optimization_barrier((dost, back))
    gq, direct = call(
        back_body, [((tokens, TILE), BF16), ((2, tokens, TILE), F32)], 10**4, 10**4, 9
    )(q, grad_rows, k, v, dost_now, m_all, inverse, delta, dqt)
    low = (me >> 1) & 1
    a_pair = jnp.stack([a_keep, a_one])
    a_stay = lax.dynamic_slice_in_dim(a_pair, low, 1, 1)[:, 0]
    a_send = lax.dynamic_slice_in_dim(a_pair, 1 - low, 1, 1)[:, 0]
    a_two = lax.ppermute(a_send, "head", by_two)
    a_two, _ = lax.optimization_barrier((a_two, back))
    mine, other = call(
        project_body, [((tokens // heads, model), F32), ((tokens // heads, model), BF16)], 10**4, 10**4, 4
    )(a_stay, a_two, w_four, w_chip)
    back, mine = lax.optimization_barrier((back, mine))
    far = lax.ppermute(back, "tm", [(c + MEM, c) for c in range(clips - MEM)])
    theirs = lax.ppermute(other, "head", by_four)
    projected = (mine + theirs.astype(F32)).astype(BF16)
    gk, gv = call(
        final_body, [((tokens, TILE), BF16), ((tokens, TILE), BF16)], 10**4, 10**4, 3
    )(direct, near, far)
    return projected[None], gq[None], gk[None], gv[None]


def solution(mesh):
    return jax.shard_map(
        local,
        mesh=mesh,
        in_specs=(
            P("tm", None, "head"),
            P("tm", None, "head"),
            P("tm", None, "head"),
            P("head", None),
            P("tm", None, None),
            P("tm"),
        ),
        out_specs=(
            P("tm", "head", None),
            P("tm", None, "head"),
            P("tm", None, "head"),
            P("tm", None, "head"),
        ),
        check_vma=False,
    )
```

```python
import jax
import jax.numpy as jnp
from jax import lax
from jax.experimental import pallas as pl
from jax.experimental.pallas import tpu as pltpu
from jax.sharding import PartitionSpec as P

HEAD_DIM = 64
POOL = 4
MEM = 8
SLOT = 112
TILE = 128
F32 = jnp.float32
BF16 = jnp.bfloat16
VMEM_LIMIT = 20 * 1024 * 1024


def dot(a, b):
    return jnp.dot(a, b, preferred_element_type=F32)


def dot_rows(a, b):
    return lax.dot_general(a, b, (((0,), (0,)), ((), ())), preferred_element_type=F32)


def dot_cols(a, b):
    return lax.dot_general(a, b, (((1,), (1,)), ((), ())), preferred_element_type=F32)


def call(body, outs, flops, moved, n_in, scalars=0, scratch=(), spaces=None, limit=VMEM_LIMIT):
    smem = pl.BlockSpec(memory_space=pltpu.SMEM)
    vmem = pl.BlockSpec(memory_space=pltpu.VMEM)
    return pl.pallas_call(
        body,
        out_shape=tuple(jax.ShapeDtypeStruct(s, d) for s, d in outs),
        in_specs=[smem] * scalars + [
            pl.BlockSpec(memory_space=space) for space in spaces or [pltpu.VMEM] * n_in
        ],
        out_specs=tuple(vmem for _ in outs),
        scratch_shapes=list(scratch),
        compiler_params=pltpu.CompilerParams(vmem_limit_bytes=limit),
        cost_estimate=pl.CostEstimate(flops=flops, bytes_accessed=moved, transcendentals=0),
    )


def pool_body(start_ref, k_hbm, v_hbm, out_ref, k_ref, v_ref, sems):
    loads = [
        pltpu.make_async_copy(k_hbm, k_ref, sems.at[0]),
        pltpu.make_async_copy(v_hbm, v_ref, sems.at[1]),
    ]
    for load in loads:
        load.start()
    tokens = k_ref.shape[0]
    pooled = tokens // POOL
    row = lax.broadcasted_iota(jnp.int32, (SLOT, tokens), 0)
    col = lax.broadcasted_iota(jnp.int32, (SLOT, tokens), 1)
    matrix = jnp.where((col >> 2) == row, 1.0 / POOL, 0.0).astype(BF16)
    flag = start_ref[0].astype(F32)
    for load in loads:
        load.wait()
    rows = lax.broadcasted_iota(jnp.int32, (SLOT, TILE), 0)
    out_ref[0] = jnp.where(rows < pooled, dot(matrix, k_ref[...]), flag).astype(BF16)
    out_ref[1] = dot(matrix, v_ref[...]).astype(BF16)


def choose_body(own_ref, prev_ref, out_ref):
    place = lax.rem(lax.axis_index("tm"), MEM)
    own = own_ref[...].astype(F32)
    prev = prev_ref[...].astype(F32)
    for k in range(MEM):
        ours = jnp.full(own.shape, place, jnp.int32) < k
        out_ref[k] = jnp.where(ours, own, prev).astype(BF16)


def stacked(x, width):
    tokens = x.shape[0]
    lane = lax.broadcasted_iota(jnp.int32, x.shape, 1)
    low = jnp.where(lane < HEAD_DIM, x, 0.0)
    high = jnp.where(lane < HEAD_DIM, 0.0, x)
    return jnp.concatenate([low, high, jnp.zeros((width - 2 * tokens, TILE), F32)], axis=0)


def unstacked(xt, tokens):
    x = xt.T
    lane = lax.broadcasted_iota(jnp.int32, (tokens, TILE), 1)
    return jnp.where(lane < HEAD_DIM, x[:tokens], x[tokens : 2 * tokens])


def prepare_body(og_ref, w_ref, grad_ref, dost_ref):
    width = dost_ref.shape[1]
    grad = dot_cols(og_ref[...], w_ref[...]).astype(BF16)
    grad_ref[...] = grad
    dost_ref[...] = stacked(grad.astype(F32), width).T.astype(BF16)


def own_body(q_ref, k_ref, v_ref, m_ref, l_ref, ot_ref):
    width = ot_ref.shape[1]
    qs = stacked(q_ref[...].astype(F32) * HEAD_DIM**-0.5, width).astype(BF16)
    scores = dot_cols(k_ref[...], qs)
    peak = jnp.max(scores, axis=0, keepdims=True)
    expo = jnp.exp(scores - peak)
    m_ref[...] = peak
    l_ref[...] = jnp.sum(expo, axis=0, keepdims=True)
    ot_ref[...] = dot_rows(v_ref[...], expo.astype(BF16))


def memory_body(
    start_ref,
    q_ref, grad_ref, mem_ref, m_ref, l_ref, dost_hbm, ot_hbm,
    pay_ref, keep_ref, give_ref, mn_ref, inv_ref, delta_ref, dqt_ref,
    s_ref, p_ref, ds_ref, mk_ref, mv_ref, qs_ref, dos_ref, dost_ref, ot_ref, sems,
):
    width = qs_ref.shape[0]
    loads = [
        pltpu.make_async_copy(dost_hbm, dost_ref, sems.at[0]),
        pltpu.make_async_copy(ot_hbm, ot_ref, sems.at[1]),
    ]
    for load in loads:
        load.start()
    qs_ref[...] = stacked(q_ref[...].astype(F32) * HEAD_DIM**-0.5, width).astype(BF16)
    dos_ref[...] = stacked(grad_ref[...].astype(F32), width).astype(BF16)
    tiles = width // TILE
    tokens = q_ref.shape[0]
    pooled = tokens // POOL
    position = lax.axis_index("tm")
    place = lax.rem(position, MEM)
    group = lax.div(position, MEM)
    started = [mem_ref[k, 0, pl.ds(96, 16), :].astype(F32)[8:16] for k in range(MEM)]
    ages = [lax.rem(place - k - 1 + 2 * MEM, MEM) for k in range(MEM)]
    own_start = start_ref[0].astype(F32)
    row = lax.broadcasted_iota(jnp.int32, (SLOT, TILE), 0)
    peaks = [None] * tiles
    for k in range(MEM):
        absent = jnp.where((group == 0) & (place <= k), 1.0, 0.0) + own_start
        blocked = jnp.full((8, TILE), absent, F32)
        for other in range(MEM):
            if other != k:
                blocked = blocked + started[other] * jnp.where(ages[other] < ages[k], 1.0, 0.0)
        mk_ref[pl.ds(k * SLOT, SLOT), :] = mem_ref[k, 0]
        mv_ref[pl.ds(k * SLOT, SLOT), :] = mem_ref[k, 1]
        scores = dot_cols(mem_ref[k, 0], qs_ref[...])
        keep = (jnp.concatenate([blocked] * (SLOT // 8), axis=0) == 0.0) & (row < pooled)
        for t in range(tiles):
            piece = jnp.where(keep, scores[:, t * TILE : (t + 1) * TILE], -1e30)
            s_ref[pl.ds(k * SLOT, SLOT), pl.ds(t * TILE, TILE)] = piece
            top = jnp.max(piece.reshape(SLOT // 8, 8, TILE), axis=0)
            peaks[t] = top if peaks[t] is None else jnp.maximum(peaks[t], top)
    for load in loads:
        load.wait()
    for t in range(tiles):
        lanes = pl.ds(t * TILE, TILE)
        own_peak = m_ref[:, lanes]
        peak = jnp.maximum(own_peak, jnp.max(peaks[t], axis=0, keepdims=True))
        total = None
        for k in range(MEM):
            rows = pl.ds(k * SLOT, SLOT)
            expo = jnp.exp(s_ref[rows, lanes] - peak)
            s_ref[rows, lanes] = expo
            part = jnp.sum(expo.reshape(SLOT // 8, 8, TILE), axis=0)
            total = part if total is None else total + part
        factor = jnp.exp(own_peak - peak)
        inverse = 1.0 / (jnp.sum(total, axis=0, keepdims=True) + l_ref[:, lanes] * factor)
        mn_ref[:, lanes] = peak
        inv_ref[:, lanes] = inverse
        for k in range(MEM):
            rows = pl.ds(k * SLOT, SLOT)
            probs = s_ref[rows, lanes] * inverse
            s_ref[rows, lanes] = probs
            p_ref[rows, lanes] = probs.astype(BF16)
        ot_ref_piece = ot_ref[:, lanes] * (factor * inverse)
        dqt_ref[:, lanes] = ot_ref_piece
    out_t = dqt_ref[...] + dot_rows(mv_ref[...], p_ref[...])
    delta = jnp.sum(out_t * dost_ref[...].astype(F32), axis=0, keepdims=True)
    delta_ref[...] = delta
    attended = unstacked(out_t, tokens)
    each = tokens // (4 * keep_ref.shape[0])
    rest = jnp.zeros((keep_ref.shape[1] - 2 * each, TILE), F32)
    pieces = []
    for part in range(2 * keep_ref.shape[0]):
        low = attended[part * each : (part + 1) * each]
        high = attended[(part + 4) * each : (part + 5) * each]
        pieces.append(jnp.concatenate([low, high, rest], axis=0))
    odd = jnp.full(pieces[0].shape, lax.rem(lax.axis_index("head"), 2), jnp.int32) == 1
    for pair in range(keep_ref.shape[0]):
        even_piece, odd_piece = pieces[2 * pair], pieces[2 * pair + 1]
        keep_ref[pair] = jnp.where(odd, odd_piece, even_piece).astype(BF16)
        give_ref[pair] = jnp.where(odd, even_piece, odd_piece).astype(BF16)
    for k in range(MEM):
        rows = pl.ds(k * SLOT, SLOT)
        grad_probs = dot(mem_ref[k, 1], dost_ref[...])
        for t in range(tiles):
            lanes = pl.ds(t * TILE, TILE)
            piece = s_ref[rows, lanes] * (grad_probs[:, t * TILE : (t + 1) * TILE] - delta_ref[:, lanes])
            ds_ref[rows, lanes] = piece.astype(BF16)
        pay_ref[k, 0] = dot(ds_ref[rows, :], qs_ref[...]).astype(BF16)
        pay_ref[k, 1] = dot(p_ref[rows, :], dos_ref[...]).astype(BF16)
    dqt_ref[...] = dot_rows(mk_ref[...], ds_ref[...])


def back_body(
    q_ref, grad_ref, k_ref, v_ref, dost_ref, m_ref, inv_ref, delta_ref, dqt_ref,
    gq_ref, own_ref,
):
    tokens = k_ref.shape[0]
    width = dost_ref.shape[1]
    qs = stacked(q_ref[...].astype(F32) * HEAD_DIM**-0.5, width).astype(BF16)
    dos = stacked(grad_ref[...].astype(F32), width).astype(BF16)
    scores = dot_cols(k_ref[...], qs)
    probs = jnp.exp(scores - m_ref[...]) * inv_ref[...]
    grad_probs = dot(v_ref[...], dost_ref[...])
    grad_scores = (probs * (grad_probs - delta_ref[...])).astype(BF16)
    own_ref[0] = dot(grad_scores, qs)
    own_ref[1] = dot(probs.astype(BF16), dos)
    grad_t = (dqt_ref[...] + dot_rows(k_ref[...], grad_scores)) * HEAD_DIM**-0.5
    gq_ref[...] = unstacked(grad_t, tokens).astype(BF16)


def sum_body(got_ref, prev_ref, own_ref):
    place = lax.rem(lax.axis_index("tm"), MEM)
    prev = jnp.zeros(own_ref.shape, F32)
    own = jnp.zeros(own_ref.shape, F32)
    for i in range(MEM):
        block = got_ref[i].astype(F32)
        share = jnp.where(i <= place, 1.0, 0.0)
        prev = prev + block * share
        own = own + block * (1.0 - share)
    prev_ref[...] = prev.astype(BF16)
    own_ref[...] = own


def final_body(direct_ref, near_ref, far_ref, gk_ref, gv_ref):
    tokens = gk_ref.shape[0]
    row = lax.broadcasted_iota(jnp.int32, (tokens, SLOT), 0)
    col = lax.broadcasted_iota(jnp.int32, (tokens, SLOT), 1)
    matrix = jnp.where((row >> 2) == col, 1.0 / POOL, 0.0).astype(BF16)
    for which, out_ref in enumerate((gk_ref, gv_ref)):
        total = near_ref[which] + far_ref[which].astype(F32)
        high = total.astype(BF16)
        low = (total - high.astype(F32)).astype(BF16)
        spread = dot(matrix, high) + dot(matrix, low)
        out_ref[...] = (direct_ref[which] + spread).astype(BF16)


def project_body(keep_ref, near_ref, w_ref, chip_ref, mine_ref, other_ref):
    upper = lax.rem(lax.axis_index("head") >> 2, 2)
    core = lax.rem(lax.axis_index("tm"), 2)
    rows = mine_ref.shape[0]
    half = w_ref.shape[1]
    total = None
    for part in range(w_ref.shape[0]):
        att = (keep_ref[part] if part < 2 else near_ref[part - 2]).astype(F32)
        swap = jnp.full(att.shape, core, jnp.int32) == 1
        att = jnp.where(swap, pltpu.roll(att, half, 1), att).astype(BF16)
        term = dot(att[:, :half], w_ref[part]) + dot(att[:, half:], chip_ref[part])
        total = term if total is None else total + term
    first, second = total[:rows], total[rows : 2 * rows]
    take = jnp.full(first.shape, upper, jnp.int32) == 1
    mine_ref[...] = jnp.where(take, second, first)
    other_ref[...] = jnp.where(take, first, second).astype(BF16)


def local(queries, key_tokens, value_tokens, out_weight, out_grad, clip_starts):
    q, k, v, grad = queries[0], key_tokens[0], value_tokens[0], out_grad[0]
    tokens = q.shape[0]
    clips = lax.axis_size("tm")
    heads = lax.axis_size("head")
    model = out_weight.shape[1]
    width = 7 * TILE
    groups = [list(range(s, s + MEM)) for s in range(0, clips, MEM)]
    me = lax.axis_index("head")
    core = lax.axis_index("tm") % 2
    half = out_weight.shape[0] // 2
    by_one, by_two, by_four = ([(h, h ^ step) for h in range(heads)] for step in (1, 2, 4))

    (own,) = call(
        pool_body, [((2, SLOT, TILE), BF16)], 10**7, 10**6, 2, 1,
        [pltpu.VMEM(k.shape, BF16), pltpu.VMEM(v.shape, BF16), pltpu.SemaphoreType.DMA((2,))],
        [pltpu.HBM] * 2, 60 * 1024 * 1024,
    )(clip_starts, k, v)
    prev = lax.ppermute(own, "tm", [(c, c + MEM) for c in range(clips - MEM)])
    grad, _ = lax.optimization_barrier((grad, own))
    grad_rows, dost = call(
        prepare_body, [((tokens, TILE), BF16), ((TILE, width), BF16)], 10**9, 2 * 10**6, 2
    )(grad, out_weight)
    w_seen, _ = lax.optimization_barrier((out_weight, own))
    w_half = lax.dynamic_slice_in_dim(w_seen, core * half, half, 0)
    w_one = lax.ppermute(w_half, "head", by_one)
    prev, grad_rows = lax.optimization_barrier((prev, grad_rows))
    (outgoing,) = call(choose_body, [((MEM, 2, SLOT, TILE), BF16)], 2 * 10**10, 10**6, 2)(own, prev)
    outgoing, w_one = lax.optimization_barrier((outgoing, w_one))
    w_pair = jnp.stack([w_half, w_one])
    memory = lax.all_to_all(outgoing, "tm", 0, 0, axis_index_groups=groups)
    q_now, _ = lax.optimization_barrier((q, outgoing))
    m_own, l_own, ot_own = call(
        own_body, [((1, width), F32), ((1, width), F32), ((TILE, width), F32)], 10**9, 10**6, 3
    )(q_now, k, v)
    w_sent, m_own = lax.optimization_barrier((w_pair, m_own))
    w_two = lax.ppermute(w_sent, "head", by_two)
    payload, a_keep, a_give, m_all, inverse, delta, dqt = call(
        memory_body,
        [
            ((MEM, 2, SLOT, TILE), BF16), ((2, SLOT, TILE), BF16), ((2, SLOT, TILE), BF16),
            ((1, width), F32), ((1, width), F32), ((1, width), F32), ((TILE, width), F32),
        ],
        4 * 10**9, 4 * 10**6, 7, 1,
        [
            pltpu.VMEM((MEM * SLOT, width), F32), pltpu.VMEM((MEM * SLOT, width), BF16),
            pltpu.VMEM((MEM * SLOT, width), BF16), pltpu.VMEM((MEM * SLOT, TILE), BF16),
            pltpu.VMEM((MEM * SLOT, TILE), BF16), pltpu.VMEM((width, TILE), BF16),
            pltpu.VMEM((width, TILE), BF16), pltpu.VMEM((TILE, width), BF16),
            pltpu.VMEM((TILE, width), F32), pltpu.SemaphoreType.DMA((2,)),
        ],
        [pltpu.VMEM] * 5 + [pltpu.HBM] * 2,
    )(clip_starts, q, grad_rows, memory, m_own, l_own, dost, ot_own)
    arrived = lax.all_to_all(payload, "tm", 0, 0, axis_index_groups=groups)
    a_one = lax.ppermute(a_give, "head", by_one)
    w_pair, w_two, _ = lax.optimization_barrier((w_pair, w_two, a_keep))
    w_four = jnp.concatenate([w_pair, w_two])
    w_chip = lax.ppermute(w_four, "tm", [(c, c ^ 1) for c in range(clips)])
    back, near = call(
        sum_body, [((2, SLOT, TILE), BF16), ((2, SLOT, TILE), F32)], 2 * 10**10, 10**6, 1
    )(arrived)
    dost_now, _ = lax.optimization_barrier((dost, back))
    gq, direct = call(
        back_body, [((tokens, TILE), BF16), ((2, tokens, TILE), F32)], 10**4, 10**4, 9
    )(q, grad_rows, k, v, dost_now, m_all, inverse, delta, dqt)
    low = (me >> 1) & 1
    a_pair = jnp.stack([a_keep, a_one])
    a_stay = lax.dynamic_slice_in_dim(a_pair, low, 1, 1)[:, 0]
    a_send = lax.dynamic_slice_in_dim(a_pair, 1 - low, 1, 1)[:, 0]
    a_two = lax.ppermute(a_send, "head", by_two)
    a_two, _ = lax.optimization_barrier((a_two, back))
    mine, other = call(
        project_body, [((tokens // heads, model), F32), ((tokens // heads, model), BF16)], 10**4, 10**4, 4
    )(a_stay, a_two, w_four, w_chip)
    back, mine = lax.optimization_barrier((back, mine))
    far = lax.ppermute(back, "tm", [(c + MEM, c) for c in range(clips - MEM)])
    theirs = lax.ppermute(other, "head", by_four)
    projected = (mine + theirs.astype(F32)).astype(BF16)
    gk, gv = call(
        final_body, [((tokens, TILE), BF16), ((tokens, TILE), BF16)], 10**4, 10**4, 3
    )(direct, near, far)
    return projected[None], gq[None], gk[None], gv[None]


def solution(mesh):
    return jax.shard_map(
        local,
        mesh=mesh,
        in_specs=(
            P("tm", None, "head"),
            P("tm", None, "head"),
            P("tm", None, "head"),
            P("head", None),
            P("tm", None, None),
            P("tm"),
        ),
        out_specs=(
            P("tm", "head", None),
            P("tm", None, "head"),
            P("tm", None, "head"),
            P("tm", None, "head"),
        ),
        check_vma=False,
    )
```
